32 devices in a mesh: tile: 8 (over z, core), chan: 4 (over y, x).
Axes of the slice: x: 2, y: 2, z: 4, core: 2. Of those that a mesh axis runs over, the one named last changes fastest.
Arguments:
- voltages: int32 [512, 131072], P('tile', 'chan'), may hold values from -128 to 127
- history: int32 [512, 30720], P('tile'), may hold values from -128 to 127
- filter_taps: int32 [16, 2048], replicated, may hold values from -64 to 64
Outputs:
- visibilities: float32 [2, 1024, 512, 512], P(None, 'chan', 'tile')
The draws below stay inside these ranges and needn't reach their ends.
Inputs may be any that keep to these rules, and one draw needn't show every extreme that they name: `voltages`: 8-bit signed samples. `history`: 8-bit signed samples.
All inputs are finite; a program needn't handle non-finite values.
Results may differ from the reference program's by a relative error of at most 0.006.
Values may be sent and summed in bfloat16 or wider, within the bound.
No kernel may reach another device: no remote copies, remote signals or barrier semaphores. Data moves between devices by JAX's collectives and lax.ppermute only.
A program may use at most 320 MiB of HBM per device.

```python
import math
import jax
import jax.numpy as jnp
from jax import lax

CH = 1024
TAPS = 16
INPUTS = 512
FFT = 2048
SPEC = 64


def plant(values, stream_key, smallest, high):
    place = [jax.random.randint(jax.random.fold_in(stream_key, axis), (), 0, length) for axis, length in enumerate(values.shape)]
    main_axis = values.shape.index(max(values.shape))
    next_to = place[:main_axis] + [(place[main_axis] + 1) % values.shape[main_axis]] + place[main_axis + 1:]
    return values.at[tuple(place)].set(smallest).at[tuple(next_to)].set(high)


def setup_inputs(seed: int = 0) -> dict:
    keys = jax.random.split(jax.random.key(seed), 4)
    return {
        "voltages": plant(jax.random.randint(keys[0], (INPUTS, SPEC * FFT), -128, 128), jax.random.fold_in(keys[0], 1), -128, 127).astype(jnp.int32),
        "history": plant(jax.random.randint(keys[1], (INPUTS, (TAPS - 1) * FFT), -128, 128), jax.random.fold_in(keys[1], 1), -128, 127).astype(jnp.int32),
        "filter_taps": plant(jax.random.randint(keys[2], (TAPS, FFT), -64, 65), jax.random.fold_in(keys[2], 1), -64, 64).astype(jnp.int32),
    }


filter_norm = 1.0 / 16384.0

def dft_table(samples, channels):
    rows_index = jnp.arange(samples, dtype=jnp.int32)[:, None]
    cols_index = jnp.arange(channels, dtype=jnp.int32)[None, :]
    angles = (rows_index * cols_index % samples).astype(jnp.float32) * (2.0 * math.pi / samples)
    factor = 1.0 / math.sqrt(channels)
    return jnp.concatenate([jnp.cos(angles) * factor, -jnp.sin(angles) * factor], axis=1).astype(jnp.bfloat16)

def polyphase(extended, weights, spectra_count):
    summed = jnp.zeros((extended.shape[0], spectra_count, extended.shape[2]), jnp.float32)
    for tap_index in range(weights.shape[0]):
        summed = summed + weights[tap_index][None, None, :] * extended[:, tap_index:tap_index + spectra_count, :]
    return summed

def counter_rows(spectra):
    real_part = spectra[:, :, 0]
    imag_part = spectra[:, :, 1]
    rotated = jnp.stack([imag_part, -real_part], axis=2)
    return jnp.stack([spectra, rotated], axis=0)

def reference(voltages, history, filter_taps):
    inputs_all = voltages.shape[0]
    spectra_count = voltages.shape[1] // FFT
    extended = jnp.concatenate([history.astype(jnp.float32), voltages.astype(jnp.float32)], axis=1)
    extended = extended.reshape(inputs_all, spectra_count + TAPS - 1, FFT)
    filtered = (polyphase(extended, filter_taps.astype(jnp.float32), spectra_count) * filter_norm).astype(jnp.bfloat16)
    spectra = jnp.dot(filtered.reshape(-1, FFT), dft_table(FFT, CH), preferred_element_type=jnp.float32)
    spectra = spectra.reshape(inputs_all, spectra_count, 2, CH).astype(jnp.bfloat16)
    width_block = math.gcd(CH, 64)
    block_count = CH // width_block
    grouped = spectra.reshape(inputs_all, spectra_count, 2, block_count, width_block).transpose(3, 0, 1, 2, 4).astype(jnp.float32)
    average = 1.0 / spectra_count

    def one_block(channel_part):
        stacked = counter_rows(channel_part)
        return jnp.einsum('qaspc,bspc->qcab', stacked, channel_part) * average
    results = lax.map(one_block, grouped)
    return results.transpose(1, 0, 2, 3, 4).reshape(2, CH, inputs_all, inputs_all)
```

```python
import functools
import math

import jax
import jax.numpy as jnp
import ml_dtypes
import numpy as np
from jax import lax
from jax.experimental import pallas as pl
from jax.experimental.pallas import tpu as pltpu
from jax.sharding import PartitionSpec as P

LANES = 128
ROWS = 16
VMEM = 48 * 1024 * 1024
FLOPS_A_MICROSECOND = 1.15e9
filter_norm = 1.0 / 16384.0


def dft_rows(samples):
    channels = samples // 2
    index = np.arange(channels, dtype=np.int64)[:, None] * np.arange(samples, dtype=np.int64)[None, :]
    angles = (index % samples).astype(np.float32) * np.float32(2.0 * math.pi / samples)
    factor = np.float32(1.0 / math.sqrt(channels))
    rows = np.concatenate([np.cos(angles) * factor, -np.sin(angles) * factor], axis=0)
    return rows.astype(ml_dtypes.bfloat16)


def params():
    return pltpu.CompilerParams(vmem_limit_bytes=VMEM)


class Order:
    def __init__(self):
        self.token = None

    def call(self, kernel, name, place, operands, in_specs, out_shape, out_specs, grid, scratch=(), after=(), aliased=(), micros=1.0):
        later = list(after) + ([] if self.token is None else [self.token])
        extra = [*aliased, *later]
        inputs, outputs = len(operands), len(out_shape)

        def wrapped(place_ref, *refs):
            outs = refs[inputs + len(extra) :]
            outs[outputs][...] = jnp.zeros_like(outs[outputs])
            kernel(place_ref, refs[:inputs], outs[:outputs], outs[outputs + 1 :])

        results = pl.pallas_call(
            wrapped,
            out_shape=[*out_shape, jax.ShapeDtypeStruct((8, LANES), jnp.float32)],
            grid_spec=pltpu.PrefetchScalarGridSpec(
                num_scalar_prefetch=1,
                grid=grid,
                in_specs=[*in_specs, *[pl.BlockSpec(memory_space=pl.ANY)] * len(extra)],
                out_specs=[*out_specs, pl.BlockSpec((8, LANES), lambda g, place: (0, 0))],
                scratch_shapes=list(scratch),
            ),
            input_output_aliases={1 + inputs + i: i for i in range(len(aliased))},
            compiler_params=params(),
            cost_estimate=pl.CostEstimate(
                flops=int(micros * FLOPS_A_MICROSECOND), bytes_accessed=0, transcendentals=0
            ),
            name=name,
        )(place, *operands, *extra)
        self.token = results[-1]
        return results[:-1]


def convert(order, place, voltages, chunk, count, parts, spectra, fft):
    each = ROWS // parts

    def kernel(place, ins, outs, scratch):
        (v_ref,), (work,), me = ins, scratch, place[0]

        def block(nb, carry):
            lane = pl.multiple_of(nb * LANES, LANES)
            for s in range(spectra):
                for top in range(0, ROWS, 8):
                    x = v_ref[top : top + 8, pl.ds(pl.multiple_of(s * fft + lane, LANES), LANES)]
                    work[pl.ds(top * spectra + s, 8, stride=spectra), :] = x.astype(jnp.float32)
            for slot in range(parts):
                for i in range(each):
                    row = pl.multiple_of(((me ^ slot) * each + i) * spectra, spectra)
                    outs[slot][0, i, :, pl.ds(lane, LANES)] = work[pl.ds(row, spectra), :].astype(jnp.bfloat16)
            return carry

        lax.fori_loop(0, fft // LANES, block, 0)

    return order.call(
        kernel,
        "convert",
        place,
        [voltages],
        [pl.BlockSpec((ROWS, spectra * fft), lambda g, place: (chunk + g, 0))],
        [jax.ShapeDtypeStruct((count, each, spectra, fft), jnp.bfloat16)] * parts,
        [pl.BlockSpec((1, each, spectra, fft), lambda g, place: (g, 0, 0, 0))] * parts,
        (count,),
        [pltpu.VMEM((ROWS * spectra, LANES), jnp.float32)],
        micros=2.5 * count,
    )


def own_history(order, place, history, parts, taps, fft):
    each = ROWS // parts
    chunks = history.shape[0] // ROWS

    def kernel(place, ins, outs, scratch):
        (h_ref,), (out,), (work,), me = ins, outs, scratch, place[0]
        work[...] = jnp.zeros_like(work)

        def block(nb, carry):
            lane = pl.multiple_of(nb * LANES, LANES)
            for s in range(taps - 1):
                x = h_ref[:, pl.ds(pl.multiple_of(s * fft + lane, LANES), LANES)]
                work[pl.ds(s + 1, 8, stride=taps), :] = x.astype(jnp.float32)
            for i in range(each):
                row = pl.multiple_of((lax.rem(me * each, 8) + i) * taps, taps)
                out[0, i, :, pl.ds(lane, LANES)] = work[pl.ds(row, taps), :].astype(jnp.bfloat16)
            return carry

        lax.fori_loop(0, fft // LANES, block, 0)

    return order.call(
        kernel,
        "history",
        place,
        [history],
        [pl.BlockSpec((8, history.shape[1]), lambda g, place: (g * (ROWS // 8) + place[0] * each // 8, 0))],
        [jax.ShapeDtypeStruct((chunks, each, taps, fft), jnp.bfloat16)],
        [pl.BlockSpec((1, each, taps, fft), lambda g, place: (g, 0, 0, 0))],
        (chunks,),
        [pltpu.VMEM((8 * taps, LANES), jnp.float32)],
        micros=4.5,
    )[0]


def channelize(order, place, filter_taps, hist, pieces, inner, table, chunk, split, after=()):
    parts = len(pieces)
    _, each, spectra, fft = pieces[0].shape
    taps = filter_taps.shape[0]
    total = parts * spectra
    channels = fft // 2 // parts

    def kernel(place, ins, outs, scratch):
        taps_ref, hist_ref, *refs = ins
        blocks, (cos_ref, sin_ref) = refs[:parts], refs[parts:]
        extended, filtered = scratch
        me, step = place[0], pl.program_id(0)

        @pl.when(step == 0)
        def _():
            def block(nb, carry):
                lane = pl.multiple_of(nb * LANES, LANES)
                columns = pl.ds(lane, LANES)
                weights = taps_ref[:, columns].astype(jnp.float32)
                for i in range(each):
                    extended[i, 0:taps, :] = hist_ref[0, i, :, columns].astype(jnp.float32)
                    for slot in range(parts):
                        row = pl.multiple_of(taps + (me ^ slot) * spectra, ROWS)
                        extended[i, pl.ds(row, spectra), :] = blocks[slot][0, i, :, columns].astype(jnp.float32)
                for i in range(each):
                    summed = weights[0:1, :] * extended[i, 1 : 1 + total, :]
                    for t in range(1, taps):
                        summed = summed + weights[t : t + 1, :] * extended[i, t + 1 : t + 1 + total, :]
                    filtered[i * total : (i + 1) * total, columns] = (summed * filter_norm).astype(jnp.bfloat16)
                return carry

            lax.fori_loop(0, fft // LANES, block, 0)

        dims = (((1,), (1,)), ((), ()))
        block = filtered[...]
        real = lax.dot_general(cos_ref[...], block, dims, preferred_element_type=jnp.float32)
        imag = lax.dot_general(sin_ref[...], block, dims, preferred_element_type=jnp.float32)
        results = []
        if 2 * total == LANES and each % 2 == 0:
            low = lax.broadcasted_iota(jnp.int32, (real.shape[0], LANES), 1) < total
            for pair in range(each // 2):
                r = real[:, pair * LANES : (pair + 1) * LANES]
                m = imag[:, pair * LANES : (pair + 1) * LANES]
                results.append(jnp.where(low, r, pltpu.roll(m, total, 1)))
                results.append(jnp.where(low, pltpu.roll(r, total, 1), m))
        else:
            for i in range(each):
                cut = slice(i * total, (i + 1) * total)
                results.append(jnp.concatenate([real[:, cut], imag[:, cut]], axis=1))
        results = [value.astype(jnp.bfloat16) for value in results]
        if not split:
            for i in range(each):
                outs[0][0, i] = results[i]
            return
        for slot in range(parts):

            @pl.when(step == slot)
            def _(slot=slot):
                for i in range(each):
                    outs[slot][i] = results[i]

    shape = (each, channels, 2 * total)
    if split:
        out_shape = [jax.ShapeDtypeStruct(shape, jnp.bfloat16)] * parts
        out_specs = [pl.BlockSpec(shape, lambda g, place: (0, 0, 0))] * parts
    else:
        out_shape = [jax.ShapeDtypeStruct((parts, *shape), jnp.bfloat16)]
        out_specs = [pl.BlockSpec((1, *shape), lambda g, place: (g, 0, 0, 0))]
    return order.call(
        kernel,
        "channelize",
        place,
        [filter_taps, hist, *pieces, table, table],
        [
            pl.BlockSpec((taps, fft), lambda g, place: (0, 0)),
            pl.BlockSpec((1, each, taps, fft), lambda g, place: (chunk, 0, 0, 0)),
            *[pl.BlockSpec((1, each, spectra, fft), lambda g, place: (inner, 0, 0, 0))] * parts,
            pl.BlockSpec((channels, fft), lambda g, place: (place[0] ^ g, 0)),
            pl.BlockSpec((channels, fft), lambda g, place: (parts + (place[0] ^ g), 0)),
        ],
        out_shape,
        out_specs,
        (parts,),
        [pltpu.VMEM((each, taps + total, LANES), jnp.float32), pltpu.VMEM((each * total, fft), jnp.bfloat16)],
        after=after,
        micros=9.0,
    )


def choose(order, place, candidates, after=()):
    parts, each, channels, width = candidates[0].shape

    def kernel(place, ins, outs, scratch):
        for which, ref in enumerate(ins):

            @pl.when(place[3] == which)
            def _(ref=ref):
                for slot in range(parts):

                    @pl.when(pl.program_id(0) == slot)
                    def _(slot=slot):
                        outs[slot][...] = ref[0]

    def spec(which):
        return pl.BlockSpec(
            (1, each, channels, width), lambda g, place: (jnp.where(place[3] == which, g, 0), 0, 0, 0)
        )

    return order.call(
        kernel,
        "choose",
        place,
        candidates,
        [spec(which) for which in range(len(candidates))],
        [jax.ShapeDtypeStruct((each, channels, width), jnp.bfloat16)] * parts,
        [pl.BlockSpec((each, channels, width), lambda g, place: (0, 0, 0))] * parts,
        (parts,),
        after=after,
    )


def merge(order, place, pieces, cuts=1, position=0, rows=ROWS, into=(), after=()):
    parts = len(pieces)
    each, channels, width = pieces[0].shape
    cut = channels // cuts

    def kernel(place, ins, outs, scratch):
        (work,), me = scratch, place[0]
        for slot in range(parts):
            for i in range(each):
                row = pl.multiple_of(((me ^ slot) * each + i) * channels, channels)
                for lane in range(0, width, LANES):
                    value = ins[slot][i, :, lane : lane + LANES]
                    work[lane // LANES, pl.ds(row, channels), :] = value.astype(jnp.float32)

        for which in range(cuts):

            def block(group, carry, which=which):
                for inner in range(8):
                    k = group * 8 + inner
                    for lane in range(0, width, LANES):
                        value = work[lane // LANES, pl.ds(which * cut + k, ROWS, stride=channels), :]
                        outs[which][k, :, lane : lane + LANES] = value.astype(jnp.bfloat16)
                return carry

            lax.fori_loop(0, cut // 8, block, 0)

    return order.call(
        kernel,
        "merge",
        place,
        pieces,
        [pl.BlockSpec((each, channels, width), lambda g, place: (0, 0, 0))] * parts,
        [jax.ShapeDtypeStruct((cut, rows, width), jnp.bfloat16)] * cuts,
        [pl.BlockSpec((cut, ROWS, width), lambda g, place: (0, position, 0))] * cuts,
        (1,),
        [pltpu.VMEM((width // LANES, ROWS * channels, LANES), jnp.float32)],
        after=after,
        aliased=into,
        micros=2.0,
    )


def turn(order, place, plain, after=()):
    channels, rows, width = plain.shape
    count = 16

    def kernel(place, ins, outs, scratch):
        low = lax.broadcasted_iota(jnp.int32, (rows, width), 1) < width // 2
        for k in range(count):
            other = pltpu.roll(ins[0][k].astype(jnp.float32), width // 2, 1)
            outs[0][k] = jnp.where(low, other, -other).astype(jnp.bfloat16)

    block = pl.BlockSpec((count, rows, width), lambda g, place: (g, 0, 0))
    shape = jax.ShapeDtypeStruct(plain.shape, jnp.bfloat16)
    return order.call(kernel, "turn", place, [plain], [block], [shape], [block], (channels // count,), after=after, micros=2.0)[0]


def correlate(order, place, out, left, sets, cut, cuts, groups, after=()):
    head, tail = left[0][0], left[0][1]
    rows_head, rows_tail, width = head.shape[1], tail.shape[1], head.shape[2]
    half = rows_head + rows_tail
    channels = head.shape[0]
    count = 16
    steps = channels // cuts // count
    average = 2.0 / width
    sizes = [len(candidates) for _, candidates in sets]

    def kernel(place, ins, outs, scratch):
        left_refs, right = ins[:4], list(ins[4:])
        (out_ref,), (columns,), core = outs, scratch, place[1]
        for s, size in enumerate(sizes):
            mine, theirs, *options = right[: 2 + 2 * size]
            del right[: 2 + 2 * size]
            base = place[2 + 2 * s] * (2 * half) if len(sizes) > 1 else 0
            first = pl.multiple_of(base + core * half, ROWS)
            second = pl.multiple_of(base + (1 - core) * half, ROWS)
            for k in range(count):
                columns[k, pl.ds(first, rows_head), :] = mine[k]
                columns[k, pl.ds(second, rows_head), :] = theirs[k]
            for which in range(size):

                @pl.when(place[3 + 2 * s] == which)
                def _(which=which, options=options, first=first, second=second):
                    for k in range(count):
                        columns[k, pl.ds(first + rows_head, rows_tail), :] = options[2 * which][k]
                        columns[k, pl.ds(second + rows_head, rows_tail), :] = options[2 * which + 1][k]

        for k in range(count):
            rows = jnp.concatenate([ref[k] for ref in left_refs], axis=0)
            result = lax.dot_general(rows, columns[k], (((1,), (1,)), ((), ())), preferred_element_type=jnp.float32)
            out_ref[0, k] = result[:half] * average
            out_ref[1, k] = result[half:] * average

    def early(g, place):
        return (cut * steps + g, 0, 0)

    def spec(s, which):
        return pl.BlockSpec((count, rows_tail, width), lambda g, place: (jnp.where(place[3 + 2 * s] == which, g, 0), 0, 0))

    head_spec = pl.BlockSpec((count, rows_head, width), early)
    tail_spec = pl.BlockSpec((count, rows_tail, width), lambda g, place: (g, 0, 0))
    operands = [left[0][0], left[0][1], left[1][0], left[1][1]]
    specs = [head_spec, tail_spec, head_spec, tail_spec]
    for s, (heads, candidates) in enumerate(sets):
        operands += heads
        specs += [head_spec] * 2
        for which, pair in enumerate(candidates):
            operands += pair
            specs += [spec(s, which)] * 2
    lanes = len(sets) * 2 * half
    if len(sets) > 1:
        out_spec = pl.BlockSpec((2, count, half, lanes), lambda g, place: (0, cut * steps + g, 0, 0))
    else:
        out_spec = pl.BlockSpec((2, count, half, lanes), lambda g, place: (0, cut * steps + g, 0, place[2]))
    return order.call(
        kernel,
        "correlate",
        place,
        operands,
        specs,
        [jax.ShapeDtypeStruct((2, channels, half, groups * 2 * half), jnp.float32)],
        [out_spec],
        (steps,),
        [pltpu.VMEM((count, lanes, width), jnp.bfloat16)],
        after=after,
        aliased=[] if out is None else [out],
        micros=10.0,
    )[0]


def exchange(pieces):
    count = len(pieces)
    return [pieces[0]] + [
        lax.ppermute(pieces[slot], "chan", [(i, i ^ slot) for i in range(count)]) for slot in range(1, count)
    ]


def body(voltages, history, filter_taps, table):
    parts = lax.axis_size("chan")
    tiles = lax.axis_size("tile")
    groups = tiles // 2
    me = lax.axis_index("chan")
    tile = lax.axis_index("tile")
    core, level = lax.rem(tile, 2), tile // 2
    taps, fft = filter_taps.shape
    spectra = voltages.shape[1] // fft
    chunks = voltages.shape[0] // ROWS
    later = (chunks - 1) * ROWS
    cuts = 2
    order = Order()

    def place(*pairs):
        return jnp.stack([jnp.asarray(x, jnp.int32) for x in (me, core, *[x for pair in pairs for x in pair])])

    def along(value, lowest, highest, step):
        pairs = [(2 * g + c, 2 * (g + step) + c) for g in range(lowest, highest + 1) for c in range(2)]
        return lax.ppermute(value, "tile", pairs)

    def hops(value):
        up, down = {0: value}, {0: value}
        for hop in range(1, groups):
            up[hop] = along(up[hop - 1], hop - 1, groups - 2, 1)
            down[hop] = along(down[hop - 1], 1, groups - hop, -1)
        return up, down

    def swap(value):
        return lax.ppermute(value, "tile", [(i, i ^ 1) for i in range(tiles)])

    here = place((level, 0))

    def pick(hop):
        below, above = level >= hop, level + hop < groups
        source = jnp.where(below, level - hop, jnp.where(above, level + hop, level + groups - hop))
        return source, jnp.where(below, 0, jnp.where(above, 1, 2))

    raw = {}

    def read(chunk, count):
        pieces = exchange(convert(order, here, voltages, chunk, count, parts, spectra, fft))
        for inner in range(count):
            raw[chunk + inner] = (pieces, inner)

    def filter_chunk(chunk, split, after=()):
        return channelize(order, here, filter_taps, hist, *raw[chunk], table, chunk, split, after)

    def arrived(hop):
        return (early_up[hop], early_down[hop]) if hop < groups else ()

    read(0, 1)
    if chunks > 1:
        read(1, 1)
    hist = own_history(order, here, history, parts, taps, fft)
    (early,) = filter_chunk(0, False)
    early_up, early_down = hops(early)
    if chunks > 2:
        read(2, chunks - 2)
    sent, plain = {}, []
    for chunk in range(1, chunks):
        sent[chunk] = exchange(filter_chunk(chunk, True, arrived(1) if chunk == chunks - 1 else ()))
        if chunk > 1:
            plain = merge(order, here, sent[chunk - 1], cuts, chunk - 2, later, plain)
    plain = merge(order, here, sent[chunks - 1], cuts, chunks - 2, later, plain, arrived(2))
    lines = [hops(value) for value in plain]

    (head,) = merge(order, here, exchange(choose(order, here, [early])))
    head_turned = turn(order, here, head, arrived(3))
    turned = [turn(order, here, value) for value in plain]
    lefts = [((head, plain[cut]), (head_turned, turned[cut])) for cut in range(cuts)]

    swapped = {}

    def both(kind, hop, cut):
        key = (kind, hop, cut)
        if key not in swapped:
            swapped[key] = swap(lines[cut][kind][hop])
        return swapped[key]

    def work(hop):
        if hop == 0:
            heads = [head, swap(head)]
            return (level, 0), [(heads, [(plain[cut], swap(plain[cut]))]) for cut in range(cuts)]
        chip = pick(hop)
        options = [(0, hop), (1, hop)] + ([(1, groups - hop)] if 2 * hop > groups else [])
        arrays = [(early_up, early_down)[kind][h] for kind, h in options]
        (own,) = merge(order, here, exchange(choose(order, place(chip), arrays)))
        heads = [own, swap(own)]
        return chip, [
            (heads, [(lines[cut][kind][h], both(kind, h, cut)) for kind, h in options]) for cut in range(cuts)
        ]

    out = None
    if 2 * voltages.shape[0] % LANES == 0:
        for hop in range(groups):
            chip, sets = work(hop)
            for cut in range(cuts):
                out = correlate(order, place(chip), out, lefts[cut], [sets[cut]], cut, cuts, groups)
    else:
        chips, sets = zip(*[work(hop) for hop in range(groups)])
        for cut in range(cuts):
            out = correlate(order, place(*chips), out, lefts[cut], [s[cut] for s in sets], cut, cuts, groups)
    return out


def solution(mesh):
    in_specs = (P("tile", "chan"), P("tile", None), P(), P())
    out_specs = P(None, "chan", "tile", None)
    mapped = jax.shard_map(body, mesh=mesh, in_specs=in_specs, out_specs=out_specs, check_vma=False)

    def run(voltages, history, filter_taps):
        return mapped(voltages, history, filter_taps, jnp.asarray(dft_rows(filter_taps.shape[1])))

    return run
```

```python
import functools
import math

import jax
import jax.numpy as jnp
import ml_dtypes
import numpy as np
from jax import lax
from jax.experimental import pallas as pl
from jax.experimental.pallas import tpu as pltpu
from jax.sharding import PartitionSpec as P

LANES = 128
ROWS = 16
VMEM = 48 * 1024 * 1024
FLOPS_A_MICROSECOND = 1.15e9
CORRELATE_MICROS = 7.0
HOP_MICROS = 40.0
filter_norm = 1.0 / 16384.0


def dft_rows(samples):
    channels = samples // 2
    index = np.arange(channels, dtype=np.int64)[:, None] * np.arange(samples, dtype=np.int64)[None, :]
    angles = (index % samples).astype(np.float32) * np.float32(2.0 * math.pi / samples)
    factor = np.float32(1.0 / math.sqrt(channels))
    rows = np.concatenate([np.cos(angles) * factor, -np.sin(angles) * factor], axis=0)
    return rows.astype(ml_dtypes.bfloat16)


def params():
    return pltpu.CompilerParams(vmem_limit_bytes=VMEM)


class Order:
    def __init__(self):
        self.token = None

    def call(self, kernel, name, place, operands, in_specs, out_shape, out_specs, grid, scratch=(), after=(), aliased=(), micros=1.0):
        later = list(after) + ([] if self.token is None else [self.token])
        extra = [*aliased, *later]
        inputs, outputs = len(operands), len(out_shape)

        def wrapped(place_ref, *refs):
            outs = refs[inputs + len(extra) :]
            outs[outputs][...] = jnp.zeros_like(outs[outputs])
            kernel(place_ref, refs[:inputs], outs[:outputs], outs[outputs + 1 :])

        results = pl.pallas_call(
            wrapped,
            out_shape=[*out_shape, jax.ShapeDtypeStruct((8, LANES), jnp.float32)],
            grid_spec=pltpu.PrefetchScalarGridSpec(
                num_scalar_prefetch=1,
                grid=grid,
                in_specs=[*in_specs, *[pl.BlockSpec(memory_space=pl.ANY)] * len(extra)],
                out_specs=[*out_specs, pl.BlockSpec((8, LANES), lambda g, place: (0, 0))],
                scratch_shapes=list(scratch),
            ),
            input_output_aliases={1 + inputs + i: i for i in range(len(aliased))},
            compiler_params=params(),
            cost_estimate=pl.CostEstimate(
                flops=int(micros * FLOPS_A_MICROSECOND), bytes_accessed=0, transcendentals=0
            ),
            name=name,
        )(place, *operands, *extra)
        self.token = results[-1]
        return results[:-1]


def convert(order, place, voltages, chunk, count, parts, spectra, fft):
    each = ROWS // parts

    def kernel(place, ins, outs, scratch):
        (v_ref,), (work,), me = ins, scratch, place[0]

        def block(nb, carry):
            lane = pl.multiple_of(nb * LANES, LANES)
            for s in range(spectra):
                for top in range(0, ROWS, 8):
                    x = v_ref[top : top + 8, pl.ds(pl.multiple_of(s * fft + lane, LANES), LANES)]
                    work[pl.ds(top * spectra + s, 8, stride=spectra), :] = x.astype(jnp.float32)
            for slot in range(parts):
                for i in range(each):
                    row = pl.multiple_of(((me ^ slot) * each + i) * spectra, spectra)
                    outs[slot][0, i, :, pl.ds(lane, LANES)] = work[pl.ds(row, spectra), :].astype(jnp.bfloat16)
            return carry

        lax.fori_loop(0, fft // LANES, block, 0)

    return order.call(
        kernel,
        "convert",
        place,
        [voltages],
        [pl.BlockSpec((ROWS, spectra * fft), lambda g, place: (chunk + g, 0))],
        [jax.ShapeDtypeStruct((count, each, spectra, fft), jnp.bfloat16)] * parts,
        [pl.BlockSpec((1, each, spectra, fft), lambda g, place: (g, 0, 0, 0))] * parts,
        (count,),
        [pltpu.VMEM((ROWS * spectra, LANES), jnp.float32)],
        micros=2.5 * count,
    )


def own_history(order, place, history, parts, taps, fft):
    each = ROWS // parts
    chunks = history.shape[0] // ROWS

    def kernel(place, ins, outs, scratch):
        (h_ref,), (out,), (work,), me = ins, outs, scratch, place[0]
        work[...] = jnp.zeros_like(work)

        def block(nb, carry):
            lane = pl.multiple_of(nb * LANES, LANES)
            for s in range(taps - 1):
                x = h_ref[:, pl.ds(pl.multiple_of(s * fft + lane, LANES), LANES)]
                work[pl.ds(s + 1, 8, stride=taps), :] = x.astype(jnp.float32)
            for i in range(each):
                row = pl.multiple_of((lax.rem(me * each, 8) + i) * taps, taps)
                out[0, i, :, pl.ds(lane, LANES)] = work[pl.ds(row, taps), :].astype(jnp.bfloat16)
            return carry

        lax.fori_loop(0, fft // LANES, block, 0)

    return order.call(
        kernel,
        "history",
        place,
        [history],
        [pl.BlockSpec((8, history.shape[1]), lambda g, place: (g * (ROWS // 8) + place[0] * each // 8, 0))],
        [jax.ShapeDtypeStruct((chunks, each, taps, fft), jnp.bfloat16)],
        [pl.BlockSpec((1, each, taps, fft), lambda g, place: (g, 0, 0, 0))],
        (chunks,),
        [pltpu.VMEM((8 * taps, LANES), jnp.float32)],
        micros=4.5,
    )[0]


def channelize(order, place, filter_taps, hist, pieces, inner, table, chunk, split, after=()):
    parts = len(pieces)
    _, each, spectra, fft = pieces[0].shape
    taps = filter_taps.shape[0]
    total = parts * spectra
    channels = fft // 2 // parts

    def kernel(place, ins, outs, scratch):
        taps_ref, hist_ref, *refs = ins
        blocks, table_ref = refs[:parts], refs[parts]
        extended, filtered, rows_of, arrived = scratch
        me = place[0]
        copies = []
        for slot in range(parts):
            for part in range(2):
                first = pl.multiple_of((part * parts + (me ^ slot)) * channels, channels)
                source, target = table_ref.at[pl.ds(first, channels), :], rows_of.at[slot, part]
                copies.append(pltpu.make_async_copy(source, target, arrived.at[slot, part]))
                copies[-1].start()

        def fill():
            def block(nb, carry):
                lane = pl.multiple_of(nb * LANES, LANES)
                columns = pl.ds(lane, LANES)
                weights = taps_ref[:, columns].astype(jnp.float32)
                for i in range(each):
                    extended[i, 0:taps, :] = hist_ref[0, i, :, columns].astype(jnp.float32)
                    for slot in range(parts):
                        row = pl.multiple_of(taps + (me ^ slot) * spectra, ROWS)
                        extended[i, pl.ds(row, spectra), :] = blocks[slot][0, i, :, columns].astype(jnp.float32)
                for i in range(each):
                    summed = weights[0:1, :] * extended[i, 1 : 1 + total, :]
                    for t in range(1, taps):
                        summed = summed + weights[t : t + 1, :] * extended[i, t + 1 : t + 1 + total, :]
                    filtered[i * total : (i + 1) * total, columns] = (summed * filter_norm).astype(jnp.bfloat16)
                return carry

            lax.fori_loop(0, fft // LANES, block, 0)

        fill()
        dims = (((1,), (1,)), ((), ()))
        block = filtered[...]
        low = lax.broadcasted_iota(jnp.int32, (channels, LANES), 1) < total
        for slot in range(parts):
            for part in range(2):
                copies[2 * slot + part].wait()
            real = lax.dot_general(rows_of[slot, 0], block, dims, preferred_element_type=jnp.float32)
            imag = lax.dot_general(rows_of[slot, 1], block, dims, preferred_element_type=jnp.float32)
            results = []
            if 2 * total == LANES and each % 2 == 0:
                for pair in range(each // 2):
                    r = real[:, pair * LANES : (pair + 1) * LANES]
                    m = imag[:, pair * LANES : (pair + 1) * LANES]
                    results.append(jnp.where(low, r, pltpu.roll(m, total, 1)))
                    results.append(jnp.where(low, pltpu.roll(r, total, 1), m))
            else:
                for i in range(each):
                    cut = slice(i * total, (i + 1) * total)
                    results.append(jnp.concatenate([real[:, cut], imag[:, cut]], axis=1))
            for i in range(each):
                value = results[i].astype(jnp.bfloat16)
                if split:
                    outs[slot][i] = value
                else:
                    outs[0][me ^ slot, i] = value

    shape = (each, channels, 2 * total)
    if split:
        out_shape = [jax.ShapeDtypeStruct(shape, jnp.bfloat16)] * parts
        out_specs = [pl.BlockSpec(shape, lambda g, place: (0, 0, 0))] * parts
    else:
        out_shape = [jax.ShapeDtypeStruct((parts, *shape), jnp.bfloat16)]
        out_specs = [pl.BlockSpec((parts, *shape), lambda g, place: (0, 0, 0, 0))]
    return order.call(
        kernel,
        "channelize",
        place,
        [filter_taps, hist, *pieces, table],
        [
            pl.BlockSpec((taps, fft), lambda g, place: (0, 0)),
            pl.BlockSpec((1, each, taps, fft), lambda g, place: (chunk, 0, 0, 0)),
            *[pl.BlockSpec((1, each, spectra, fft), lambda g, place: (inner, 0, 0, 0))] * parts,
            pl.BlockSpec(memory_space=pl.ANY),
        ],
        out_shape,
        out_specs,
        (1,),
        [
            pltpu.VMEM((each, taps + total, LANES), jnp.float32),
            pltpu.VMEM((each * total, fft), jnp.bfloat16),
            pltpu.VMEM((parts, 2, channels, fft), jnp.bfloat16),
            pltpu.SemaphoreType.DMA((parts, 2)),
        ],
        after=after,
        micros=9.0,
    )


def select(order, place, candidates, after=()):
    channels, rows, width = candidates[0].shape
    count = channels // 4

    def kernel(place, ins, outs, scratch):
        for which, ref in enumerate(ins):

            @pl.when(place[4] == which)
            def _(ref=ref):
                outs[0][...] = ref[...]

    def spec(which):
        return pl.BlockSpec((count, rows, width), lambda g, place: (jnp.where(place[4] == which, g, 0), 0, 0))

    return order.call(
        kernel,
        "select",
        place,
        candidates,
        [spec(which) for which in range(len(candidates))],
        [jax.ShapeDtypeStruct((channels, rows, width), jnp.bfloat16)],
        [pl.BlockSpec((count, rows, width), lambda g, place: (g, 0, 0))],
        (channels // count,),
        after=after,
    )[0]


def merge(order, place, pieces, cuts=1, position=0, rows=ROWS, into=(), after=()):
    parts = len(pieces)
    each, channels, width = pieces[0].shape
    cut = channels // cuts

    def kernel(place, ins, outs, scratch):
        (work,), me = scratch, place[0]
        for slot in range(parts):
            for i in range(each):
                row = pl.multiple_of(((me ^ slot) * each + i) * channels, channels)
                for lane in range(0, width, LANES):
                    value = ins[slot][i, :, lane : lane + LANES]
                    work[lane // LANES, pl.ds(row, channels), :] = value.astype(jnp.float32)

        for which in range(cuts):

            def block(group, carry, which=which):
                for inner in range(8):
                    k = group * 8 + inner
                    for lane in range(0, width, LANES):
                        value = work[lane // LANES, pl.ds(which * cut + k, ROWS, stride=channels), :]
                        outs[which][k, :, lane : lane + LANES] = value.astype(jnp.bfloat16)
                return carry

            lax.fori_loop(0, cut // 8, block, 0)

    return order.call(
        kernel,
        "merge",
        place,
        pieces,
        [pl.BlockSpec((each, channels, width), lambda g, place: (0, 0, 0))] * parts,
        [jax.ShapeDtypeStruct((cut, rows, width), jnp.bfloat16)] * cuts,
        [pl.BlockSpec((cut, ROWS, width), lambda g, place: (0, position, 0))] * cuts,
        (1,),
        [pltpu.VMEM((width // LANES, ROWS * channels, LANES), jnp.float32)],
        after=after,
        aliased=into,
        micros=2.0,
    )


def gate(order, place, values, after=(), micros=0.1):
    return order.call(
        lambda place, ins, outs, scratch: None,
        "gate",
        place,
        [],
        [],
        [jax.ShapeDtypeStruct(value.shape, value.dtype) for value in values],
        [pl.BlockSpec(memory_space=pl.ANY)] * len(values),
        (1,),
        after=after,
        aliased=values,
        micros=micros,
    )


def merge_early(order, place, pieces, after=()):
    parts, groups, each, channels, width = pieces.shape

    def kernel(place, ins, outs, scratch):
        (work,) = scratch
        for source in range(parts):
            for i in range(each):
                rows = slice((source * each + i) * channels, (source * each + i + 1) * channels)
                for lane in range(0, width, LANES):
                    work[lane // LANES, rows, :] = ins[0][source, 0, i, :, lane : lane + LANES].astype(jnp.float32)

        def block(group, carry):
            for inner in range(8):
                k = group * 8 + inner
                for lane in range(0, width, LANES):
                    value = work[lane // LANES, pl.ds(k, ROWS, stride=channels), :]
                    outs[0][0, k, :, lane : lane + LANES] = value.astype(jnp.bfloat16)
            return carry

        lax.fori_loop(0, channels // 8, block, 0)

    return order.call(
        kernel,
        "merge_early",
        place,
        [pieces],
        [pl.BlockSpec((parts, 1, each, channels, width), lambda g, place: (0, g, 0, 0, 0))],
        [jax.ShapeDtypeStruct((groups, channels, ROWS, width), jnp.bfloat16)],
        [pl.BlockSpec((1, channels, ROWS, width), lambda g, place: (g, 0, 0, 0))],
        (groups,),
        [pltpu.VMEM((width // LANES, ROWS * channels, LANES), jnp.float32)],
        after=after,
        micros=HOP_MICROS,
    )[0]


def turn(order, place, plain, after=()):
    channels, rows, width = plain.shape[-3:]
    stacked = plain.ndim == 4
    count = 16

    def kernel(place, ins, outs, scratch):
        low = lax.broadcasted_iota(jnp.int32, (rows, width), 1) < width // 2
        for k in range(count):
            value = ins[0][0, k] if stacked else ins[0][k]
            other = pltpu.roll(value.astype(jnp.float32), width // 2, 1)
            outs[0][k] = jnp.where(low, other, -other).astype(jnp.bfloat16)

    block = pl.BlockSpec((count, rows, width), lambda g, place: (g, 0, 0))
    source = pl.BlockSpec((1, count, rows, width), lambda g, place: (place[2], g, 0, 0)) if stacked else block
    shape = jax.ShapeDtypeStruct((channels, rows, width), jnp.bfloat16)
    return order.call(kernel, "turn", place, [plain], [source], [shape], [block], (channels // count,), after=after, micros=0.1)[0]


def correlate(order, place, out, left, sets, cut, cuts, groups, after=(), micros=CORRELATE_MICROS):
    head, tail = left[1][0], left[0][1]
    rows_head, rows_tail, width = head.shape[1], tail.shape[1], head.shape[2]
    half = rows_head + rows_tail
    channels = head.shape[0]
    count = 32
    steps = channels // cuts // count
    average = 2.0 / width
    sizes = [len(candidates) for _, candidates in sets]

    def kernel(place, ins, outs, scratch):
        left_refs, right = ins[:4], list(ins[4:])
        (out_ref,), (columns,), core = outs, scratch, place[1]
        for s, size in enumerate(sizes):
            mine, theirs, *options = right[: 2 + 2 * size]
            del right[: 2 + 2 * size]
            base = place[3 + 2 * s] * (2 * half) if len(sizes) > 1 else 0
            first = pl.multiple_of(base + core * half, ROWS)
            second = pl.multiple_of(base + (1 - core) * half, ROWS)
            for k in range(count):
                columns[k, pl.ds(first, rows_head), :] = mine[0, k]
                columns[k, pl.ds(second, rows_head), :] = theirs[0, k]
            for which in range(size):

                @pl.when(place[4 + 2 * s] == which)
                def _(which=which, options=options, first=first, second=second):
                    for k in range(count):
                        columns[k, pl.ds(first + rows_head, rows_tail), :] = options[2 * which][k]
                        columns[k, pl.ds(second + rows_head, rows_tail), :] = options[2 * which + 1][k]

        for k in range(count):
            rows = [left_refs[0][0, k], *[ref[k] for ref in left_refs[1:]]]
            rows = jnp.concatenate(rows, axis=0)
            result = lax.dot_general(rows, columns[k], (((1,), (1,)), ((), ())), preferred_element_type=jnp.float32)
            out_ref[0, k] = result[:half] * average
            out_ref[1, k] = result[half:] * average

    def early(g, place):
        return (cut * steps + g, 0, 0)

    def spec(s, which):
        return pl.BlockSpec((count, rows_tail, width), lambda g, place: (jnp.where(place[4 + 2 * s] == which, g, 0), 0, 0))

    def early_of(s):
        return pl.BlockSpec(
            (1, count, rows_head, width), lambda g, place: (place[2 if s is None else 3 + 2 * s], cut * steps + g, 0, 0)
        )

    head_spec = pl.BlockSpec((count, rows_head, width), early)
    tail_spec = pl.BlockSpec((count, rows_tail, width), lambda g, place: (g, 0, 0))
    operands = [left[0][0], left[0][1], left[1][0], left[1][1]]
    specs = [early_of(None), tail_spec, head_spec, tail_spec]
    for s, (heads, candidates) in enumerate(sets):
        operands += heads
        specs += [early_of(s)] * 2
        for which, pair in enumerate(candidates):
            operands += pair
            specs += [spec(s, which)] * 2
    lanes = len(sets) * 2 * half
    if len(sets) > 1:
        out_spec = pl.BlockSpec((2, count, half, lanes), lambda g, place: (0, cut * steps + g, 0, 0))
    else:
        out_spec = pl.BlockSpec((2, count, half, lanes), lambda g, place: (0, cut * steps + g, 0, place[3]))
    return order.call(
        kernel,
        "correlate",
        place,
        operands,
        specs,
        [jax.ShapeDtypeStruct((2, channels, half, groups * 2 * half), jnp.float32)],
        [out_spec],
        (steps,),
        [pltpu.VMEM((count, lanes, width), jnp.bfloat16)],
        after=after,
        aliased=[] if out is None else [out],
        micros=micros,
    )[0]


def exchange(pieces):
    count = len(pieces)
    return [pieces[0]] + [
        lax.ppermute(pieces[slot], "chan", [(i, i ^ slot) for i in range(count)]) for slot in range(1, count)
    ]


def body(voltages, history, filter_taps, table):
    parts = lax.axis_size("chan")
    tiles = lax.axis_size("tile")
    groups = tiles // 2
    me = lax.axis_index("chan")
    tile = lax.axis_index("tile")
    core, level = lax.rem(tile, 2), tile // 2
    taps, fft = filter_taps.shape
    spectra = voltages.shape[1] // fft
    chunks = voltages.shape[0] // ROWS
    later = (chunks - 1) * ROWS
    cuts = 2
    order = Order()

    def place(*pairs):
        return jnp.stack([jnp.asarray(x, jnp.int32) for x in (me, core, level, *[x for pair in pairs for x in pair])])

    def along(value, lowest, highest, step):
        pairs = [(2 * g + c, 2 * (g + step) + c) for g in range(lowest, highest + 1) for c in range(2)]
        return lax.ppermute(value, "tile", pairs)

    def swap(value):
        return lax.ppermute(value, "tile", [(i, i ^ 1) for i in range(tiles)])

    here = place()

    middle = (groups + 1) // 2

    def pick(hop):
        below, above = level >= hop, level + hop < groups
        source = jnp.where(below, level - hop, jnp.where(above, level + hop, level + groups - hop))
        if hop < middle:
            return source, jnp.where(below, 0, 1)
        return source, jnp.where(jnp.logical_or(below, above), 0, 1)

    raw = {}

    def read(chunk, count):
        pieces = exchange(convert(order, here, voltages, chunk, count, parts, spectra, fft))
        for inner in range(count):
            raw[chunk + inner] = (pieces, inner)

    def filter_chunk(chunk, split):
        return channelize(order, here, filter_taps, hist, *raw[chunk], table, chunk, split)

    read(0, 1)
    if chunks > 1:
        read(1, 1)
    hist = own_history(order, here, history, parts, taps, fft)
    if chunks > 2:
        read(2, chunks - 2)
    (early,) = filter_chunk(0, False)
    early = lax.all_gather(
        early, "tile", axis_index_groups=[[2 * group + which for group in range(groups)] for which in range(2)]
    )
    sent, plain = {}, []
    for chunk in range(1, chunks):
        sent[chunk] = exchange(filter_chunk(chunk, True))
        if chunk > 1:
            plain = merge(order, here, sent[chunk - 1], cuts, chunk - 2, later, plain)
    plain = merge(order, here, sent[chunks - 1], cuts, chunks - 2, later, plain)
    lines = [({0: value}, {0: value}) for value in plain]

    def step(hop, cut):
        up, down = lines[cut]
        if hop <= middle:
            up[hop] = along(up[hop - 1], hop - 1, groups - 2, 1)
            down[hop] = along(down[hop - 1], 1, groups - hop, -1)
        else:
            pairs = [(g, g + 1) for g in range(hop - 1, groups - 1)] + [(g, g - 1) for g in range(1, groups - hop + 1)]
            up[hop] = lax.ppermute(up[hop - 1], "tile", [(2 * g + c, 2 * h + c) for g, h in pairs for c in range(2)])

    def one_side(hop, cut):
        up, down = lines[cut]
        if hop == middle:
            up[hop] = select(order, place((level, jnp.where(level >= hop, 0, 1))), [up[hop], down[hop]])

    for cut in range(cuts):
        step(1, cut)

    (early,) = gate(order, here, [early])
    early = lax.all_to_all(jnp.swapaxes(early, 0, 1), "chan", split_axis=0, concat_axis=0, tiled=True)
    gate(order, here, [], [lines[cut][kind][1] for cut in range(cuts) for kind in range(2)], micros=HOP_MICROS)
    early = merge_early(order, here, early)
    heads = [early, swap(early)]
    turned = [turn(order, here, value) for value in plain]
    head_turned = turn(order, here, early)
    lefts = [((early, plain[cut]), (head_turned, turned[cut])) for cut in range(cuts)]

    swapped = {}

    def both(key, value):
        if key not in swapped:
            swapped[key] = swap(value)
        return value, swapped[key]

    def chip_of(hop):
        return pick(hop) if hop > 0 else (level, 0)

    def later_of(hop, cut):
        if hop == 0:
            return [both((0, 0, cut), plain[cut])]
        if hop < middle:
            return [both((kind, hop, cut), lines[cut][kind][hop]) for kind in range(2)]
        result = [both((0, hop, cut), lines[cut][0][hop])]
        if hop > groups - hop:
            result.append(both((1, groups - hop, cut), lines[cut][1][groups - hop]))
        return result

    out = None
    if 2 * voltages.shape[0] % LANES == 0:

        def write(out, hop, cut, after=()):
            sets = [(heads, later_of(hop, cut))]
            micros = CORRELATE_MICROS if hop > 0 else 1.0
            return correlate(order, place(chip_of(hop)), out, lefts[cut], sets, cut, cuts, groups, after, micros)

        for cut in range(cuts):
            out = write(out, 0, cut)
        for hop in range(1, groups):
            for cut in range(cuts):
                ahead = []
                if hop + 1 < groups:
                    step(hop + 1, cut)
                    if hop + 1 == middle:
                        one_side(hop + 1, cut)
                    elif hop + 2 < groups or cut == 0:
                        ahead = [lines[cut][0][hop + 1]]
                elif cut > 0:
                    (lines[cut][0][hop],) = gate(order, here, [lines[cut][0][hop]])
                out = write(out, hop, cut, ahead)
    else:
        for hop in range(2, groups):
            for cut in range(cuts):
                step(hop, cut)
                one_side(hop, cut)
        chips = [chip_of(hop) for hop in range(groups)]
        for cut in range(cuts):
            sets = [(heads, later_of(hop, cut)) for hop in range(groups)]
            out = correlate(order, place(*chips), out, lefts[cut], sets, cut, cuts, groups)
    return out


def solution(mesh):
    in_specs = (P("tile", "chan"), P("tile", None), P(), P())
    out_specs = P(None, "chan", "tile", None)
    mapped = jax.shard_map(body, mesh=mesh, in_specs=in_specs, out_specs=out_specs, check_vma=False)

    def run(voltages, history, filter_taps):
        return mapped(voltages, history, filter_taps, jnp.asarray(dft_rows(filter_taps.shape[1])))

    return run
```

```python
import functools
import math

import jax
import jax.numpy as jnp
import ml_dtypes
import numpy as np
from jax import lax
from jax.experimental import pallas as pl
from jax.experimental.pallas import tpu as pltpu
from jax.sharding import PartitionSpec as P

LANES = 128
ROWS = 16
VMEM = 48 * 1024 * 1024
FLOPS_A_MICROSECOND = 1.15e9
CORRELATE_MICROS = 7.0
HOP_MICROS = 40.0
filter_norm = 1.0 / 16384.0


def dft_rows(samples):
    channels = samples // 2
    index = np.arange(channels, dtype=np.int64)[:, None] * np.arange(samples, dtype=np.int64)[None, :]
    angles = (index % samples).astype(np.float32) * np.float32(2.0 * math.pi / samples)
    factor = np.float32(1.0 / math.sqrt(channels))
    rows = np.concatenate([np.cos(angles) * factor, -np.sin(angles) * factor], axis=0)
    return rows.astype(ml_dtypes.bfloat16)


def params():
    return pltpu.CompilerParams(vmem_limit_bytes=VMEM)


class Order:
    def __init__(self):
        self.token = None

    def call(self, kernel, name, place, operands, in_specs, out_shape, out_specs, grid, scratch=(), after=(), aliased=(), micros=1.0):
        later = list(after) + ([] if self.token is None else [self.token])
        extra = [*aliased, *later]
        inputs, outputs = len(operands), len(out_shape)

        def wrapped(place_ref, *refs):
            outs = refs[inputs + len(extra) :]
            outs[outputs][...] = jnp.zeros_like(outs[outputs])
            kernel(place_ref, refs[:inputs], outs[:outputs], outs[outputs + 1 :])

        results = pl.pallas_call(
            wrapped,
            out_shape=[*out_shape, jax.ShapeDtypeStruct((8, LANES), jnp.float32)],
            grid_spec=pltpu.PrefetchScalarGridSpec(
                num_scalar_prefetch=1,
                grid=grid,
                in_specs=[*in_specs, *[pl.BlockSpec(memory_space=pl.ANY)] * len(extra)],
                out_specs=[*out_specs, pl.BlockSpec((8, LANES), lambda g, place: (0, 0))],
                scratch_shapes=list(scratch),
            ),
            input_output_aliases={1 + inputs + i: i for i in range(len(aliased))},
            compiler_params=params(),
            cost_estimate=pl.CostEstimate(
                flops=int(micros * FLOPS_A_MICROSECOND), bytes_accessed=0, transcendentals=0
            ),
            name=name,
        )(place, *operands, *extra)
        self.token = results[-1]
        return results[:-1]


def convert(order, place, voltages, chunk, count, parts, spectra, fft):
    each = ROWS // parts

    def kernel(place, ins, outs, scratch):
        (v_ref,), (work,), me = ins, scratch, place[0]

        def block(nb, carry):
            lane = pl.multiple_of(nb * LANES, LANES)
            for s in range(spectra):
                for top in range(0, ROWS, 8):
                    x = v_ref[top : top + 8, pl.ds(pl.multiple_of(s * fft + lane, LANES), LANES)]
                    work[pl.ds(top * spectra + s, 8, stride=spectra), :] = x.astype(jnp.float32)
            for slot in range(parts):
                for i in range(each):
                    row = pl.multiple_of(((me ^ slot) * each + i) * spectra, spectra)
                    outs[slot][0, i, :, pl.ds(lane, LANES)] = work[pl.ds(row, spectra), :].astype(jnp.bfloat16)
            return carry

        lax.fori_loop(0, fft // LANES, block, 0)

    return order.call(
        kernel,
        "convert",
        place,
        [voltages],
        [pl.BlockSpec((ROWS, spectra * fft), lambda g, place: (chunk + g, 0))],
        [jax.ShapeDtypeStruct((count, each, spectra, fft), jnp.bfloat16)] * parts,
        [pl.BlockSpec((1, each, spectra, fft), lambda g, place: (g, 0, 0, 0))] * parts,
        (count,),
        [pltpu.VMEM((ROWS * spectra, LANES), jnp.float32)],
        micros=2.5 * count,
    )


def own_history(order, place, history, parts, taps, fft):
    each = ROWS // parts
    chunks = history.shape[0] // ROWS

    def kernel(place, ins, outs, scratch):
        (h_ref,), (out,), (work,), me = ins, outs, scratch, place[0]
        work[...] = jnp.zeros_like(work)

        def block(nb, carry):
            lane = pl.multiple_of(nb * LANES, LANES)
            for s in range(taps - 1):
                x = h_ref[:, pl.ds(pl.multiple_of(s * fft + lane, LANES), LANES)]
                work[pl.ds(s + 1, 8, stride=taps), :] = x.astype(jnp.float32)
            for i in range(each):
                row = pl.multiple_of((lax.rem(me * each, 8) + i) * taps, taps)
                out[0, i, :, pl.ds(lane, LANES)] = work[pl.ds(row, taps), :].astype(jnp.bfloat16)
            return carry

        lax.fori_loop(0, fft // LANES, block, 0)

    return order.call(
        kernel,
        "history",
        place,
        [history],
        [pl.BlockSpec((8, history.shape[1]), lambda g, place: (g * (ROWS // 8) + place[0] * each // 8, 0))],
        [jax.ShapeDtypeStruct((chunks, each, taps, fft), jnp.bfloat16)],
        [pl.BlockSpec((1, each, taps, fft), lambda g, place: (g, 0, 0, 0))],
        (chunks,),
        [pltpu.VMEM((8 * taps, LANES), jnp.float32)],
        micros=4.5,
    )[0]


def channelize(order, place, filter_taps, hist, pieces, inner, table, chunk, split, after=()):
    parts = len(pieces)
    _, each, spectra, fft = pieces[0].shape
    taps = filter_taps.shape[0]
    total = parts * spectra
    channels = fft // 2 // parts

    def kernel(place, ins, outs, scratch):
        taps_ref, hist_ref, *refs = ins
        blocks, table_ref = refs[:parts], refs[parts]
        extended, filtered, rows_of, arrived = scratch
        me = place[0]
        copies = []
        for slot in range(parts):
            for part in range(2):
                first = pl.multiple_of((part * parts + (me ^ slot)) * channels, channels)
                source, target = table_ref.at[pl.ds(first, channels), :], rows_of.at[slot, part]
                copies.append(pltpu.make_async_copy(source, target, arrived.at[slot, part]))
                copies[-1].start()

        def fill():
            def block(nb, carry):
                lane = pl.multiple_of(nb * LANES, LANES)
                columns = pl.ds(lane, LANES)
                weights = taps_ref[:, columns].astype(jnp.float32)
                for i in range(each):
                    extended[i, 0:taps, :] = hist_ref[0, i, :, columns].astype(jnp.float32)
                    for slot in range(parts):
                        row = pl.multiple_of(taps + (me ^ slot) * spectra, ROWS)
                        extended[i, pl.ds(row, spectra), :] = blocks[slot][0, i, :, columns].astype(jnp.float32)
                for i in range(each):
                    summed = weights[0:1, :] * extended[i, 1 : 1 + total, :]
                    for t in range(1, taps):
                        summed = summed + weights[t : t + 1, :] * extended[i, t + 1 : t + 1 + total, :]
                    filtered[i * total : (i + 1) * total, columns] = (summed * filter_norm).astype(jnp.bfloat16)
                return carry

            lax.fori_loop(0, fft // LANES, block, 0)

        fill()
        dims = (((1,), (1,)), ((), ()))
        block = filtered[...]
        low = lax.broadcasted_iota(jnp.int32, (channels, LANES), 1) < total
        for slot in range(parts):
            for part in range(2):
                copies[2 * slot + part].wait()
            real = lax.dot_general(rows_of[slot, 0], block, dims, preferred_element_type=jnp.float32)
            imag = lax.dot_general(rows_of[slot, 1], block, dims, preferred_element_type=jnp.float32)
            results = []
            if 2 * total == LANES and each % 2 == 0:
                for pair in range(each // 2):
                    r = real[:, pair * LANES : (pair + 1) * LANES]
                    m = imag[:, pair * LANES : (pair + 1) * LANES]
                    results.append(jnp.where(low, r, pltpu.roll(m, total, 1)))
                    results.append(jnp.where(low, pltpu.roll(r, total, 1), m))
            else:
                for i in range(each):
                    cut = slice(i * total, (i + 1) * total)
                    results.append(jnp.concatenate([real[:, cut], imag[:, cut]], axis=1))
            for i in range(each):
                value = results[i].astype(jnp.bfloat16)
                if split:
                    outs[slot][i] = value
                else:
                    outs[0][me ^ slot, i] = value

    shape = (each, channels, 2 * total)
    if split:
        out_shape = [jax.ShapeDtypeStruct(shape, jnp.bfloat16)] * parts
        out_specs = [pl.BlockSpec(shape, lambda g, place: (0, 0, 0))] * parts
    else:
        out_shape = [jax.ShapeDtypeStruct((parts, *shape), jnp.bfloat16)]
        out_specs = [pl.BlockSpec((parts, *shape), lambda g, place: (0, 0, 0, 0))]
    return order.call(
        kernel,
        "channelize",
        place,
        [filter_taps, hist, *pieces, table],
        [
            pl.BlockSpec((taps, fft), lambda g, place: (0, 0)),
            pl.BlockSpec((1, each, taps, fft), lambda g, place: (chunk, 0, 0, 0)),
            *[pl.BlockSpec((1, each, spectra, fft), lambda g, place: (inner, 0, 0, 0))] * parts,
            pl.BlockSpec(memory_space=pl.ANY),
        ],
        out_shape,
        out_specs,
        (1,),
        [
            pltpu.VMEM((each, taps + total, LANES), jnp.float32),
            pltpu.VMEM((each * total, fft), jnp.bfloat16),
            pltpu.VMEM((parts, 2, channels, fft), jnp.bfloat16),
            pltpu.SemaphoreType.DMA((parts, 2)),
        ],
        after=after,
        micros=9.0,
    )


def select(order, place, candidates, after=()):
    channels, rows, width = candidates[0].shape
    count = channels // 4

    def kernel(place, ins, outs, scratch):
        for which, ref in enumerate(ins):

            @pl.when(place[4] == which)
            def _(ref=ref):
                outs[0][...] = ref[...]

    def spec(which):
        return pl.BlockSpec((count, rows, width), lambda g, place: (jnp.where(place[4] == which, g, 0), 0, 0))

    return order.call(
        kernel,
        "select",
        place,
        candidates,
        [spec(which) for which in range(len(candidates))],
        [jax.ShapeDtypeStruct((channels, rows, width), jnp.bfloat16)],
        [pl.BlockSpec((count, rows, width), lambda g, place: (g, 0, 0))],
        (channels // count,),
        after=after,
    )[0]


def merge(order, place, pieces, cuts=1, position=0, rows=ROWS, into=(), after=()):
    parts = len(pieces)
    each, channels, width = pieces[0].shape
    cut = channels // cuts

    def kernel(place, ins, outs, scratch):
        (work,), me = scratch, place[0]
        for slot in range(parts):
            for i in range(each):
                row = pl.multiple_of(((me ^ slot) * each + i) * channels, channels)
                for lane in range(0, width, LANES):
                    value = ins[slot][i, :, lane : lane + LANES]
                    work[lane // LANES, pl.ds(row, channels), :] = value.astype(jnp.float32)

        for which in range(cuts):

            def block(group, carry, which=which):
                for inner in range(8):
                    k = group * 8 + inner
                    for lane in range(0, width, LANES):
                        value = work[lane // LANES, pl.ds(which * cut + k, ROWS, stride=channels), :]
                        outs[which][k, :, lane : lane + LANES] = value.astype(jnp.bfloat16)
                return carry

            lax.fori_loop(0, cut // 8, block, 0)

    return order.call(
        kernel,
        "merge",
        place,
        pieces,
        [pl.BlockSpec((each, channels, width), lambda g, place: (0, 0, 0))] * parts,
        [jax.ShapeDtypeStruct((cut, rows, width), jnp.bfloat16)] * cuts,
        [pl.BlockSpec((cut, ROWS, width), lambda g, place: (0, position, 0))] * cuts,
        (1,),
        [pltpu.VMEM((width // LANES, ROWS * channels, LANES), jnp.float32)],
        after=after,
        aliased=into,
        micros=2.0,
    )


def gate(order, place, values, after=(), micros=0.1):
    return order.call(
        lambda place, ins, outs, scratch: None,
        "gate",
        place,
        [],
        [],
        [jax.ShapeDtypeStruct(value.shape, value.dtype) for value in values],
        [pl.BlockSpec(memory_space=pl.ANY)] * len(values),
        (1,),
        after=after,
        aliased=values,
        micros=micros,
    )


def merge_early(order, place, pieces, after=()):
    parts, groups, each, channels, width = pieces.shape

    def kernel(place, ins, outs, scratch):
        (work,) = scratch
        for source in range(parts):
            for i in range(each):
                rows = slice((source * each + i) * channels, (source * each + i + 1) * channels)
                for lane in range(0, width, LANES):
                    work[lane // LANES, rows, :] = ins[0][source, 0, i, :, lane : lane + LANES].astype(jnp.float32)

        def block(group, carry):
            for inner in range(8):
                k = group * 8 + inner
                for lane in range(0, width, LANES):
                    value = work[lane // LANES, pl.ds(k, ROWS, stride=channels), :]
                    outs[0][0, k, :, lane : lane + LANES] = value.astype(jnp.bfloat16)
            return carry

        lax.fori_loop(0, channels // 8, block, 0)

    return order.call(
        kernel,
        "merge_early",
        place,
        [pieces],
        [pl.BlockSpec((parts, 1, each, channels, width), lambda g, place: (0, g, 0, 0, 0))],
        [jax.ShapeDtypeStruct((groups, channels, ROWS, width), jnp.bfloat16)],
        [pl.BlockSpec((1, channels, ROWS, width), lambda g, place: (g, 0, 0, 0))],
        (groups,),
        [pltpu.VMEM((width // LANES, ROWS * channels, LANES), jnp.float32)],
        after=after,
        micros=HOP_MICROS,
    )[0]


def turn(order, place, plain, after=()):
    channels, rows, width = plain.shape[-3:]
    stacked = plain.ndim == 4
    count = 16

    def kernel(place, ins, outs, scratch):
        low = lax.broadcasted_iota(jnp.int32, (rows, width), 1) < width // 2
        for k in range(count):
            value = ins[0][0, k] if stacked else ins[0][k]
            other = pltpu.roll(value.astype(jnp.float32), width // 2, 1)
            outs[0][k] = jnp.where(low, other, -other).astype(jnp.bfloat16)

    block = pl.BlockSpec((count, rows, width), lambda g, place: (g, 0, 0))
    source = pl.BlockSpec((1, count, rows, width), lambda g, place: (place[2], g, 0, 0)) if stacked else block
    shape = jax.ShapeDtypeStruct((channels, rows, width), jnp.bfloat16)
    return order.call(kernel, "turn", place, [plain], [source], [shape], [block], (channels // count,), after=after, micros=0.1)[0]


def correlate(order, place, out, left, sets, cut, cuts, groups, after=(), micros=CORRELATE_MICROS):
    head, tail = left[1][0], left[0][1]
    rows_head, rows_tail, width = head.shape[1], tail.shape[1], head.shape[2]
    half = rows_head + rows_tail
    channels = head.shape[0]
    count = 32
    steps = channels // cuts // count
    average = 2.0 / width
    sizes = [len(candidates) for _, candidates in sets]

    def kernel(place, ins, outs, scratch):
        left_refs, right = ins[:4], list(ins[4:])
        (out_ref,), (columns,), core = outs, scratch, place[1]
        for s, size in enumerate(sizes):
            mine, theirs, *options = right[: 2 + 2 * size]
            del right[: 2 + 2 * size]
            base = place[3 + 2 * s] * (2 * half) if len(sizes) > 1 else 0
            first = pl.multiple_of(base + core * half, ROWS)
            second = pl.multiple_of(base + (1 - core) * half, ROWS)
            for k in range(count):
                columns[k, pl.ds(first, rows_head), :] = mine[0, k]
                columns[k, pl.ds(second, rows_head), :] = theirs[0, k]
            for which in range(size):

                @pl.when(place[4 + 2 * s] == which)
                def _(which=which, options=options, first=first, second=second):
                    for k in range(count):
                        columns[k, pl.ds(first + rows_head, rows_tail), :] = options[2 * which][k]
                        columns[k, pl.ds(second + rows_head, rows_tail), :] = options[2 * which + 1][k]

        for k in range(count):
            rows = [left_refs[0][0, k], *[ref[k] for ref in left_refs[1:]]]
            rows = jnp.concatenate(rows, axis=0)
            result = lax.dot_general(rows, columns[k], (((1,), (1,)), ((), ())), preferred_element_type=jnp.float32)
            out_ref[0, k] = result[:half] * average
            out_ref[1, k] = result[half:] * average

    def early(g, place):
        return (cut * steps + g, 0, 0)

    def spec(s, which):
        return pl.BlockSpec((count, rows_tail, width), lambda g, place: (jnp.where(place[4 + 2 * s] == which, g, 0), 0, 0))

    def early_of(s):
        return pl.BlockSpec(
            (1, count, rows_head, width), lambda g, place: (place[2 if s is None else 3 + 2 * s], cut * steps + g, 0, 0)
        )

    head_spec = pl.BlockSpec((count, rows_head, width), early)
    tail_spec = pl.BlockSpec((count, rows_tail, width), lambda g, place: (g, 0, 0))
    operands = [left[0][0], left[0][1], left[1][0], left[1][1]]
    specs = [early_of(None), tail_spec, head_spec, tail_spec]
    for s, (heads, candidates) in enumerate(sets):
        operands += heads
        specs += [early_of(s)] * 2
        for which, pair in enumerate(candidates):
            operands += pair
            specs += [spec(s, which)] * 2
    lanes = len(sets) * 2 * half
    if len(sets) > 1:
        out_spec = pl.BlockSpec((2, count, half, lanes), lambda g, place: (0, cut * steps + g, 0, 0))
    else:
        out_spec = pl.BlockSpec((2, count, half, lanes), lambda g, place: (0, cut * steps + g, 0, place[3]))
    return order.call(
        kernel,
        "correlate",
        place,
        operands,
        specs,
        [jax.ShapeDtypeStruct((2, channels, half, groups * 2 * half), jnp.float32)],
        [out_spec],
        (steps,),
        [pltpu.VMEM((count, lanes, width), jnp.bfloat16)],
        after=after,
        aliased=[] if out is None else [out],
        micros=micros,
    )[0]


def exchange(pieces):
    count = len(pieces)
    return [pieces[0]] + [
        lax.ppermute(pieces[slot], "chan", [(i, i ^ slot) for i in range(count)]) for slot in range(1, count)
    ]


def body(voltages, history, filter_taps, table):
    parts = lax.axis_size("chan")
    tiles = lax.axis_size("tile")
    groups = tiles // 2
    me = lax.axis_index("chan")
    tile = lax.axis_index("tile")
    core, level = lax.rem(tile, 2), tile // 2
    taps, fft = filter_taps.shape
    spectra = voltages.shape[1] // fft
    chunks = voltages.shape[0] // ROWS
    later = (chunks - 1) * ROWS
    cuts = 2
    order = Order()

    def place(*pairs):
        return jnp.stack([jnp.asarray(x, jnp.int32) for x in (me, core, level, *[x for pair in pairs for x in pair])])

    def along(value, lowest, highest, step):
        pairs = [(2 * g + c, 2 * (g + step) + c) for g in range(lowest, highest + 1) for c in range(2)]
        return lax.ppermute(value, "tile", pairs)

    def swap(value):
        return lax.ppermute(value, "tile", [(i, i ^ 1) for i in range(tiles)])

    here = place()

    middle = (groups + 1) // 2

    def pick(hop):
        below, above = level >= hop, level + hop < groups
        source = jnp.where(below, level - hop, jnp.where(above, level + hop, level + groups - hop))
        if hop < middle:
            return source, jnp.where(below, 0, 1)
        return source, jnp.where(jnp.logical_or(below, above), 0, 1)

    raw = {}

    def read(chunk, count):
        pieces = exchange(convert(order, here, voltages, chunk, count, parts, spectra, fft))
        for inner in range(count):
            raw[chunk + inner] = (pieces, inner)

    def filter_chunk(chunk, split):
        return channelize(order, here, filter_taps, hist, *raw[chunk], table, chunk, split)

    read(0, 1)
    if chunks > 1:
        read(1, 1)
    hist = own_history(order, here, history, parts, taps, fft)
    if chunks > 2:
        read(2, chunks - 2)
    (early,) = filter_chunk(0, False)
    early = lax.all_gather(
        early, "tile", axis_index_groups=[[2 * group + which for group in range(groups)] for which in range(2)]
    )
    sent, plain = {}, []
    for chunk in range(1, chunks):
        sent[chunk] = exchange(filter_chunk(chunk, True))
        if chunk > 1:
            plain = merge(order, here, sent[chunk - 1], cuts, chunk - 2, later, plain)
    plain = merge(order, here, sent[chunks - 1], cuts, chunks - 2, later, plain)
    lines = [({0: value}, {0: value}) for value in plain]

    def step(hop, cut):
        up, down = lines[cut]
        if hop <= middle:
            up[hop] = along(up[hop - 1], hop - 1, groups - 2, 1)
            down[hop] = along(down[hop - 1], 1, groups - hop, -1)
        else:
            pairs = [(g, g + 1) for g in range(hop - 1, groups - 1)] + [(g, g - 1) for g in range(1, groups - hop + 1)]
            up[hop] = lax.ppermute(up[hop - 1], "tile", [(2 * g + c, 2 * h + c) for g, h in pairs for c in range(2)])

    def one_side(hop, cut):
        up, down = lines[cut]
        if hop == middle:
            up[hop] = select(order, place((level, jnp.where(level >= hop, 0, 1))), [up[hop], down[hop]])

    for cut in range(cuts):
        step(1, cut)

    (early,) = gate(order, here, [early])
    early = lax.all_to_all(jnp.swapaxes(early, 0, 1), "chan", split_axis=0, concat_axis=0, tiled=True)
    gate(order, here, [], [lines[cut][kind][1] for cut in range(cuts) for kind in range(2)], micros=HOP_MICROS)
    other = swap(early)
    early = merge_early(order, here, early)
    heads = [early, merge_early(order, here, other)]
    turned = [turn(order, here, value) for value in plain]
    head_turned = turn(order, here, early)
    lefts = [((early, plain[cut]), (head_turned, turned[cut])) for cut in range(cuts)]

    swapped = {}

    def both(key, value):
        if key not in swapped:
            swapped[key] = swap(value)
        return value, swapped[key]

    def chip_of(hop):
        return pick(hop) if hop > 0 else (level, 0)

    def later_of(hop, cut):
        if hop == 0:
            return [both((0, 0, cut), plain[cut])]
        if hop < middle:
            return [both((kind, hop, cut), lines[cut][kind][hop]) for kind in range(2)]
        result = [both((0, hop, cut), lines[cut][0][hop])]
        if hop > groups - hop:
            result.append(both((1, groups - hop, cut), lines[cut][1][groups - hop]))
        return result

    out = None
    if 2 * voltages.shape[0] % LANES == 0:

        def write(out, hop, cut, after=()):
            sets = [(heads, later_of(hop, cut))]
            micros = CORRELATE_MICROS if hop > 0 else 1.0
            return correlate(order, place(chip_of(hop)), out, lefts[cut], sets, cut, cuts, groups, after, micros)

        for cut in range(cuts):
            out = write(out, 0, cut)
        for hop in range(1, groups):
            for cut in range(cuts):
                ahead = []
                if hop + 1 < groups:
                    step(hop + 1, cut)
                    if hop + 1 == middle:
                        one_side(hop + 1, cut)
                    elif hop + 2 < groups or cut == 0:
                        ahead = [lines[cut][0][hop + 1]]
                elif cut > 0:
                    (lines[cut][0][hop],) = gate(order, here, [lines[cut][0][hop]])
                out = write(out, hop, cut, ahead)
    else:
        for hop in range(2, groups):
            for cut in range(cuts):
                step(hop, cut)
                one_side(hop, cut)
        chips = [chip_of(hop) for hop in range(groups)]
        for cut in range(cuts):
            sets = [(heads, later_of(hop, cut)) for hop in range(groups)]
            out = correlate(order, place(*chips), out, lefts[cut], sets, cut, cuts, groups)
    return out


def solution(mesh):
    in_specs = (P("tile", "chan"), P("tile", None), P(), P())
    out_specs = P(None, "chan", "tile", None)
    mapped = jax.shard_map(body, mesh=mesh, in_specs=in_specs, out_specs=out_specs, check_vma=False)

    def run(voltages, history, filter_taps):
        return mapped(voltages, history, filter_taps, jnp.asarray(dft_rows(filter_taps.shape[1])))

    return run
```

```python
import functools
import math

import jax
import jax.numpy as jnp
import ml_dtypes
import numpy as np
from jax import lax
from jax.experimental import pallas as pl
from jax.experimental.pallas import tpu as pltpu
from jax.sharding import PartitionSpec as P

LANES = 128
ROWS = 16
VMEM = 48 * 1024 * 1024
FLOPS_A_MICROSECOND = 1.15e9
CORRELATE_MICROS = 7.0
HOP_MICROS = 40.0
filter_norm = 1.0 / 16384.0


def dft_rows(samples):
    channels = samples // 2
    index = np.arange(channels, dtype=np.int64)[:, None] * np.arange(samples, dtype=np.int64)[None, :]
    angles = (index % samples).astype(np.float32) * np.float32(2.0 * math.pi / samples)
    factor = np.float32(1.0 / math.sqrt(channels))
    rows = np.concatenate([np.cos(angles) * factor, -np.sin(angles) * factor], axis=0)
    return rows.astype(ml_dtypes.bfloat16)


def params():
    return pltpu.CompilerParams(vmem_limit_bytes=VMEM)


class Order:
    def __init__(self):
        self.token = None

    def call(self, kernel, name, place, operands, in_specs, out_shape, out_specs, grid, scratch=(), after=(), aliased=(), micros=1.0):
        later = list(after) + ([] if self.token is None else [self.token])
        extra = [*aliased, *later]
        inputs, outputs = len(operands), len(out_shape)

        def wrapped(place_ref, *refs):
            outs = refs[inputs + len(extra) :]
            outs[outputs][...] = jnp.zeros_like(outs[outputs])
            kernel(place_ref, refs[:inputs], outs[:outputs], outs[outputs + 1 :])

        results = pl.pallas_call(
            wrapped,
            out_shape=[*out_shape, jax.ShapeDtypeStruct((8, LANES), jnp.float32)],
            grid_spec=pltpu.PrefetchScalarGridSpec(
                num_scalar_prefetch=1,
                grid=grid,
                in_specs=[*in_specs, *[pl.BlockSpec(memory_space=pl.ANY)] * len(extra)],
                out_specs=[*out_specs, pl.BlockSpec((8, LANES), lambda g, place: (0, 0))],
                scratch_shapes=list(scratch),
            ),
            input_output_aliases={1 + inputs + i: i for i in range(len(aliased))},
            compiler_params=params(),
            cost_estimate=pl.CostEstimate(
                flops=int(micros * FLOPS_A_MICROSECOND), bytes_accessed=0, transcendentals=0
            ),
            name=name,
        )(place, *operands, *extra)
        self.token = results[-1]
        return results[:-1]


def convert(order, place, voltages, chunk, count, parts, spectra, fft):
    each = ROWS // parts

    def kernel(place, ins, outs, scratch):
        (v_ref,), (work,), me = ins, scratch, place[0]

        def block(nb, carry):
            lane = pl.multiple_of(nb * LANES, LANES)
            for s in range(spectra):
                for top in range(0, ROWS, 8):
                    x = v_ref[top : top + 8, pl.ds(pl.multiple_of(s * fft + lane, LANES), LANES)]
                    work[pl.ds(top * spectra + s, 8, stride=spectra), :] = x.astype(jnp.float32)
            for slot in range(parts):
                for i in range(each):
                    row = pl.multiple_of(((me ^ slot) * each + i) * spectra, spectra)
                    outs[slot][0, i, :, pl.ds(lane, LANES)] = work[pl.ds(row, spectra), :].astype(jnp.bfloat16)
            return carry

        lax.fori_loop(0, fft // LANES, block, 0)

    return order.call(
        kernel,
        "convert",
        place,
        [voltages],
        [pl.BlockSpec((ROWS, spectra * fft), lambda g, place: (chunk + g, 0))],
        [jax.ShapeDtypeStruct((count, each, spectra, fft), jnp.bfloat16)] * parts,
        [pl.BlockSpec((1, each, spectra, fft), lambda g, place: (g, 0, 0, 0))] * parts,
        (count,),
        [pltpu.VMEM((ROWS * spectra, LANES), jnp.float32)],
        micros=2.5 * count,
    )


def own_history(order, place, history, parts, taps, fft):
    each = ROWS // parts
    chunks = history.shape[0] // ROWS

    def kernel(place, ins, outs, scratch):
        (h_ref,), (out,), (work,), me = ins, outs, scratch, place[0]
        work[...] = jnp.zeros_like(work)

        def block(nb, carry):
            lane = pl.multiple_of(nb * LANES, LANES)
            for s in range(taps - 1):
                x = h_ref[:, pl.ds(pl.multiple_of(s * fft + lane, LANES), LANES)]
                work[pl.ds(s + 1, 8, stride=taps), :] = x.astype(jnp.float32)
            for i in range(each):
                row = pl.multiple_of((lax.rem(me * each, 8) + i) * taps, taps)
                out[0, i, :, pl.ds(lane, LANES)] = work[pl.ds(row, taps), :].astype(jnp.bfloat16)
            return carry

        lax.fori_loop(0, fft // LANES, block, 0)

    return order.call(
        kernel,
        "history",
        place,
        [history],
        [pl.BlockSpec((8, history.shape[1]), lambda g, place: (g * (ROWS // 8) + place[0] * each // 8, 0))],
        [jax.ShapeDtypeStruct((chunks, each, taps, fft), jnp.bfloat16)],
        [pl.BlockSpec((1, each, taps, fft), lambda g, place: (g, 0, 0, 0))],
        (chunks,),
        [pltpu.VMEM((8 * taps, LANES), jnp.float32)],
        micros=4.5,
    )[0]


def channelize(order, place, filter_taps, hist, pieces, inner, table, chunk, split, after=()):
    parts = len(pieces)
    _, each, spectra, fft = pieces[0].shape
    taps = filter_taps.shape[0]
    total = parts * spectra
    channels = fft // 2 // parts

    def kernel(place, ins, outs, scratch):
        taps_ref, hist_ref, *refs = ins
        blocks, table_ref = refs[:parts], refs[parts]
        extended, filtered, rows_of, arrived = scratch
        me = place[0]
        copies = []
        for slot in range(parts):
            for part in range(2):
                first = pl.multiple_of((part * parts + (me ^ slot)) * channels, channels)
                source, target = table_ref.at[pl.ds(first, channels), :], rows_of.at[slot, part]
                copies.append(pltpu.make_async_copy(source, target, arrived.at[slot, part]))
                copies[-1].start()

        def fill():
            def block(nb, carry):
                lane = pl.multiple_of(nb * LANES, LANES)
                columns = pl.ds(lane, LANES)
                weights = taps_ref[:, columns].astype(jnp.float32)
                for i in range(each):
                    extended[i, 0:taps, :] = hist_ref[0, i, :, columns].astype(jnp.float32)
                    for slot in range(parts):
                        row = pl.multiple_of(taps + (me ^ slot) * spectra, ROWS)
                        extended[i, pl.ds(row, spectra), :] = blocks[slot][0, i, :, columns].astype(jnp.float32)
                for i in range(each):
                    summed = weights[0:1, :] * extended[i, 1 : 1 + total, :]
                    for t in range(1, taps):
                        summed = summed + weights[t : t + 1, :] * extended[i, t + 1 : t + 1 + total, :]
                    filtered[i * total : (i + 1) * total, columns] = (summed * filter_norm).astype(jnp.bfloat16)
                return carry

            lax.fori_loop(0, fft // LANES, block, 0)

        fill()
        dims = (((1,), (1,)), ((), ()))
        block = filtered[...]
        low = lax.broadcasted_iota(jnp.int32, (channels, LANES), 1) < total
        for slot in range(parts):
            for part in range(2):
                copies[2 * slot + part].wait()
            real = lax.dot_general(rows_of[slot, 0], block, dims, preferred_element_type=jnp.float32)
            imag = lax.dot_general(rows_of[slot, 1], block, dims, preferred_element_type=jnp.float32)
            results = []
            if 2 * total == LANES and each % 2 == 0:
                for pair in range(each // 2):
                    r = real[:, pair * LANES : (pair + 1) * LANES]
                    m = imag[:, pair * LANES : (pair + 1) * LANES]
                    results.append(jnp.where(low, r, pltpu.roll(m, total, 1)))
                    results.append(jnp.where(low, pltpu.roll(r, total, 1), m))
            else:
                for i in range(each):
                    cut = slice(i * total, (i + 1) * total)
                    results.append(jnp.concatenate([real[:, cut], imag[:, cut]], axis=1))
            for i in range(each):
                value = results[i].astype(jnp.bfloat16)
                if split:
                    outs[slot][i] = value
                else:
                    outs[0][me ^ slot, i] = value

    shape = (each, channels, 2 * total)
    if split:
        out_shape = [jax.ShapeDtypeStruct(shape, jnp.bfloat16)] * parts
        out_specs = [pl.BlockSpec(shape, lambda g, place: (0, 0, 0))] * parts
    else:
        out_shape = [jax.ShapeDtypeStruct((parts, *shape), jnp.bfloat16)]
        out_specs = [pl.BlockSpec((parts, *shape), lambda g, place: (0, 0, 0, 0))]
    return order.call(
        kernel,
        "channelize",
        place,
        [filter_taps, hist, *pieces, table],
        [
            pl.BlockSpec((taps, fft), lambda g, place: (0, 0)),
            pl.BlockSpec((1, each, taps, fft), lambda g, place: (chunk, 0, 0, 0)),
            *[pl.BlockSpec((1, each, spectra, fft), lambda g, place: (inner, 0, 0, 0))] * parts,
            pl.BlockSpec(memory_space=pl.ANY),
        ],
        out_shape,
        out_specs,
        (1,),
        [
            pltpu.VMEM((each, taps + total, LANES), jnp.float32),
            pltpu.VMEM((each * total, fft), jnp.bfloat16),
            pltpu.VMEM((parts, 2, channels, fft), jnp.bfloat16),
            pltpu.SemaphoreType.DMA((parts, 2)),
        ],
        after=after,
        micros=9.0,
    )


def select(order, place, candidates, after=()):
    channels, rows, width = candidates[0].shape
    count = channels // 4

    def kernel(place, ins, outs, scratch):
        for which, ref in enumerate(ins):

            @pl.when(place[4] == which)
            def _(ref=ref):
                outs[0][...] = ref[...]

    def spec(which):
        return pl.BlockSpec((count, rows, width), lambda g, place: (jnp.where(place[4] == which, g, 0), 0, 0))

    return order.call(
        kernel,
        "select",
        place,
        candidates,
        [spec(which) for which in range(len(candidates))],
        [jax.ShapeDtypeStruct((channels, rows, width), jnp.bfloat16)],
        [pl.BlockSpec((count, rows, width), lambda g, place: (g, 0, 0))],
        (channels // count,),
        after=after,
    )[0]


def merge(order, place, pieces, cuts=1, position=0, rows=ROWS, into=(), after=()):
    parts = len(pieces)
    each, channels, width = pieces[0].shape
    cut = channels // cuts

    def kernel(place, ins, outs, scratch):
        (work,), me = scratch, place[0]
        for slot in range(parts):
            for i in range(each):
                row = pl.multiple_of(((me ^ slot) * each + i) * channels, channels)
                for lane in range(0, width, LANES):
                    value = ins[slot][i, :, lane : lane + LANES]
                    work[lane // LANES, pl.ds(row, channels), :] = value.astype(jnp.float32)

        for which in range(cuts):

            def block(group, carry, which=which):
                for inner in range(8):
                    k = group * 8 + inner
                    for lane in range(0, width, LANES):
                        value = work[lane // LANES, pl.ds(which * cut + k, ROWS, stride=channels), :]
                        outs[which][k, :, lane : lane + LANES] = value.astype(jnp.bfloat16)
                return carry

            lax.fori_loop(0, cut // 8, block, 0)

    return order.call(
        kernel,
        "merge",
        place,
        pieces,
        [pl.BlockSpec((each, channels, width), lambda g, place: (0, 0, 0))] * parts,
        [jax.ShapeDtypeStruct((cut, rows, width), jnp.bfloat16)] * cuts,
        [pl.BlockSpec((cut, ROWS, width), lambda g, place: (0, position, 0))] * cuts,
        (1,),
        [pltpu.VMEM((width // LANES, ROWS * channels, LANES), jnp.float32)],
        after=after,
        aliased=into,
        micros=2.0,
    )


def gate(order, place, values, after=(), micros=0.1):
    return order.call(
        lambda place, ins, outs, scratch: None,
        "gate",
        place,
        [],
        [],
        [jax.ShapeDtypeStruct(value.shape, value.dtype) for value in values],
        [pl.BlockSpec(memory_space=pl.ANY)] * len(values),
        (1,),
        after=after,
        aliased=values,
        micros=micros,
    )


def merge_early(order, place, pieces, after=()):
    parts, groups, each, channels, width = pieces.shape

    def kernel(place, ins, outs, scratch):
        (work,) = scratch
        for source in range(parts):
            for i in range(each):
                rows = slice((source * each + i) * channels, (source * each + i + 1) * channels)
                for lane in range(0, width, LANES):
                    work[lane // LANES, rows, :] = ins[0][source, 0, i, :, lane : lane + LANES].astype(jnp.float32)

        def block(group, carry):
            for inner in range(8):
                k = group * 8 + inner
                for lane in range(0, width, LANES):
                    value = work[lane // LANES, pl.ds(k, ROWS, stride=channels), :]
                    outs[0][0, k, :, lane : lane + LANES] = value.astype(jnp.bfloat16)
            return carry

        lax.fori_loop(0, channels // 8, block, 0)

    return order.call(
        kernel,
        "merge_early",
        place,
        [pieces],
        [pl.BlockSpec((parts, 1, each, channels, width), lambda g, place: (0, g, 0, 0, 0))],
        [jax.ShapeDtypeStruct((groups, channels, ROWS, width), jnp.bfloat16)],
        [pl.BlockSpec((1, channels, ROWS, width), lambda g, place: (g, 0, 0, 0))],
        (groups,),
        [pltpu.VMEM((width // LANES, ROWS * channels, LANES), jnp.float32)],
        after=after,
        micros=HOP_MICROS,
    )[0]


def turn(order, place, plain, after=()):
    channels, rows, width = plain.shape[-3:]
    stacked = plain.ndim == 4
    count = 16

    def kernel(place, ins, outs, scratch):
        low = lax.broadcasted_iota(jnp.int32, (rows, width), 1) < width // 2
        for k in range(count):
            value = ins[0][0, k] if stacked else ins[0][k]
            other = pltpu.roll(value.astype(jnp.float32), width // 2, 1)
            outs[0][k] = jnp.where(low, other, -other).astype(jnp.bfloat16)

    block = pl.BlockSpec((count, rows, width), lambda g, place: (g, 0, 0))
    source = pl.BlockSpec((1, count, rows, width), lambda g, place: (place[2], g, 0, 0)) if stacked else block
    shape = jax.ShapeDtypeStruct((channels, rows, width), jnp.bfloat16)
    return order.call(kernel, "turn", place, [plain], [source], [shape], [block], (channels // count,), after=after, micros=0.1)[0]


def correlate(order, place, out, left, sets, cut, cuts, groups, after=(), micros=CORRELATE_MICROS):
    head, tail = left[1][0], left[0][1]
    rows_head, rows_tail, width = head.shape[1], tail.shape[1], head.shape[2]
    half = rows_head + rows_tail
    channels = head.shape[0]
    count = 32
    steps = channels // cuts // count
    average = 2.0 / width
    sizes = [len(candidates) for _, candidates in sets]

    def kernel(place, ins, outs, scratch):
        left_refs, right = ins[:4], list(ins[4:])
        (out_ref,), (columns,), core = outs, scratch, place[1]
        for s, size in enumerate(sizes):
            mine, theirs, *options = right[: 2 + 2 * size]
            del right[: 2 + 2 * size]
            base = place[3 + 2 * s] * (2 * half) if len(sizes) > 1 else 0
            first = pl.multiple_of(base + core * half, ROWS)
            second = pl.multiple_of(base + (1 - core) * half, ROWS)
            for k in range(count):
                columns[k, pl.ds(first, rows_head), :] = mine[0, k]
                columns[k, pl.ds(second, rows_head), :] = theirs[0, k]
            for which in range(size):

                @pl.when(place[4 + 2 * s] == which)
                def _(which=which, options=options, first=first, second=second):
                    for k in range(count):
                        columns[k, pl.ds(first + rows_head, rows_tail), :] = options[2 * which][k]
                        columns[k, pl.ds(second + rows_head, rows_tail), :] = options[2 * which + 1][k]

        for k in range(count):
            rows = [left_refs[0][0, k], *[ref[k] for ref in left_refs[1:]]]
            rows = jnp.concatenate(rows, axis=0)
            result = lax.dot_general(rows, columns[k], (((1,), (1,)), ((), ())), preferred_element_type=jnp.float32)
            out_ref[0, k] = result[:half] * average
            out_ref[1, k] = result[half:] * average

    def early(g, place):
        return (cut * steps + g, 0, 0)

    def spec(s, which):
        return pl.BlockSpec((count, rows_tail, width), lambda g, place: (jnp.where(place[4 + 2 * s] == which, g, 0), 0, 0))

    def early_of(s):
        return pl.BlockSpec(
            (1, count, rows_head, width), lambda g, place: (place[2 if s is None else 3 + 2 * s], cut * steps + g, 0, 0)
        )

    head_spec = pl.BlockSpec((count, rows_head, width), early)
    tail_spec = pl.BlockSpec((count, rows_tail, width), lambda g, place: (g, 0, 0))
    operands = [left[0][0], left[0][1], left[1][0], left[1][1]]
    specs = [early_of(None), tail_spec, head_spec, tail_spec]
    for s, (heads, candidates) in enumerate(sets):
        operands += heads
        specs += [early_of(s)] * 2
        for which, pair in enumerate(candidates):
            operands += pair
            specs += [spec(s, which)] * 2
    lanes = len(sets) * 2 * half
    if len(sets) > 1:
        out_spec = pl.BlockSpec((2, count, half, lanes), lambda g, place: (0, cut * steps + g, 0, 0))
    else:
        out_spec = pl.BlockSpec((2, count, half, lanes), lambda g, place: (0, cut * steps + g, 0, place[3]))
    return order.call(
        kernel,
        "correlate",
        place,
        operands,
        specs,
        [jax.ShapeDtypeStruct((2, channels, half, groups * 2 * half), jnp.float32)],
        [out_spec],
        (steps,),
        [pltpu.VMEM((count, lanes, width), jnp.bfloat16)],
        after=after,
        aliased=[] if out is None else [out],
        micros=micros,
    )[0]


def exchange(pieces):
    count = len(pieces)
    return [pieces[0]] + [
        lax.ppermute(pieces[slot], "chan", [(i, i ^ slot) for i in range(count)]) for slot in range(1, count)
    ]


def body(voltages, history, filter_taps, table):
    parts = lax.axis_size("chan")
    tiles = lax.axis_size("tile")
    groups = tiles // 2
    me = lax.axis_index("chan")
    tile = lax.axis_index("tile")
    core, level = lax.rem(tile, 2), tile // 2
    taps, fft = filter_taps.shape
    spectra = voltages.shape[1] // fft
    chunks = voltages.shape[0] // ROWS
    later = (chunks - 1) * ROWS
    cuts = 2
    order = Order()

    def place(*pairs):
        return jnp.stack([jnp.asarray(x, jnp.int32) for x in (me, core, level, *[x for pair in pairs for x in pair])])

    def along(value, lowest, highest, step):
        pairs = [(2 * g + c, 2 * (g + step) + c) for g in range(lowest, highest + 1) for c in range(2)]
        return lax.ppermute(value, "tile", pairs)

    def swap(value):
        return lax.ppermute(value, "tile", [(i, i ^ 1) for i in range(tiles)])

    here = place()

    middle = (groups + 1) // 2

    def pick(hop):
        below, above = level >= hop, level + hop < groups
        source = jnp.where(below, level - hop, jnp.where(above, level + hop, level + groups - hop))
        if hop < middle:
            return source, jnp.where(below, 0, 1)
        return source, jnp.where(jnp.logical_or(below, above), 0, 1)

    raw = {}

    def read(chunk, count):
        pieces = exchange(convert(order, here, voltages, chunk, count, parts, spectra, fft))
        for inner in range(count):
            raw[chunk + inner] = (pieces, inner)

    def filter_chunk(chunk, split):
        return channelize(order, here, filter_taps, hist, *raw[chunk], table, chunk, split)

    read(0, 1)
    if chunks > 1:
        read(1, 1)
    hist = own_history(order, here, history, parts, taps, fft)
    (early,) = filter_chunk(0, False)
    early = lax.all_gather(
        early, "tile", axis_index_groups=[[2 * group + which for group in range(groups)] for which in range(2)]
    )
    if chunks > 2:
        read(2, chunks - 2)
    sent, plain = {}, []
    for chunk in range(1, chunks):
        sent[chunk] = exchange(filter_chunk(chunk, True))
        if chunk > 1:
            plain = merge(order, here, sent[chunk - 1], cuts, chunk - 2, later, plain)
    plain = merge(order, here, sent[chunks - 1], cuts, chunks - 2, later, plain)
    lines = [({0: value}, {0: value}) for value in plain]

    def step(hop, cut):
        up, down = lines[cut]
        if hop <= middle:
            up[hop] = along(up[hop - 1], hop - 1, groups - 2, 1)
            down[hop] = along(down[hop - 1], 1, groups - hop, -1)
        else:
            pairs = [(g, g + 1) for g in range(hop - 1, groups - 1)] + [(g, g - 1) for g in range(1, groups - hop + 1)]
            up[hop] = lax.ppermute(up[hop - 1], "tile", [(2 * g + c, 2 * h + c) for g, h in pairs for c in range(2)])

    def one_side(hop, cut):
        up, down = lines[cut]
        if hop == middle:
            up[hop] = select(order, place((level, jnp.where(level >= hop, 0, 1))), [up[hop], down[hop]])

    for cut in range(cuts):
        step(1, cut)

    (early,) = gate(order, here, [early])
    early = lax.all_to_all(jnp.swapaxes(early, 0, 1), "chan", split_axis=0, concat_axis=0, tiled=True)
    gate(order, here, [], [lines[cut][kind][1] for cut in range(cuts) for kind in range(2)], micros=HOP_MICROS)
    other = swap(early)
    early = merge_early(order, here, early)
    heads = [early, merge_early(order, here, other)]
    turned = [turn(order, here, value) for value in plain]
    head_turned = turn(order, here, early)
    lefts = [((early, plain[cut]), (head_turned, turned[cut])) for cut in range(cuts)]

    swapped = {}

    def both(key, value):
        if key not in swapped:
            swapped[key] = swap(value)
        return value, swapped[key]

    def chip_of(hop):
        return pick(hop) if hop > 0 else (level, 0)

    def later_of(hop, cut):
        if hop == 0:
            return [both((0, 0, cut), plain[cut])]
        if hop < middle:
            return [both((kind, hop, cut), lines[cut][kind][hop]) for kind in range(2)]
        result = [both((0, hop, cut), lines[cut][0][hop])]
        if hop > groups - hop:
            result.append(both((1, groups - hop, cut), lines[cut][1][groups - hop]))
        return result

    out = None
    if 2 * voltages.shape[0] % LANES == 0:

        def write(out, hop, cut, after=()):
            sets = [(heads, later_of(hop, cut))]
            micros = CORRELATE_MICROS if hop > 0 else 1.0
            return correlate(order, place(chip_of(hop)), out, lefts[cut], sets, cut, cuts, groups, after, micros)

        for cut in range(cuts):
            out = write(out, 0, cut)
        for hop in range(1, groups):
            for cut in range(cuts):
                ahead = []
                if hop + 1 < groups:
                    step(hop + 1, cut)
                    if hop + 1 == middle:
                        one_side(hop + 1, cut)
                    elif hop + 2 < groups or cut == 0:
                        ahead = [lines[cut][0][hop + 1]]
                elif cut > 0:
                    (lines[cut][0][hop],) = gate(order, here, [lines[cut][0][hop]])
                out = write(out, hop, cut, ahead)
    else:
        for hop in range(2, groups):
            for cut in range(cuts):
                step(hop, cut)
                one_side(hop, cut)
        chips = [chip_of(hop) for hop in range(groups)]
        for cut in range(cuts):
            sets = [(heads, later_of(hop, cut)) for hop in range(groups)]
            out = correlate(order, place(*chips), out, lefts[cut], sets, cut, cuts, groups)
    return out


def solution(mesh):
    in_specs = (P("tile", "chan"), P("tile", None), P(), P())
    out_specs = P(None, "chan", "tile", None)
    mapped = jax.shard_map(body, mesh=mesh, in_specs=in_specs, out_specs=out_specs, check_vma=False)

    def run(voltages, history, filter_taps):
        return mapped(voltages, history, filter_taps, jnp.asarray(dft_rows(filter_taps.shape[1])))

    return run
```
